128 devices in a mesh: tm: 16 (over x, y_lo, core), sta: 8 (over y_hi, z).
Axes of the slice: x: 4, y: 4 (y_hi: 2, y_lo: 2; y = y_hi * 2 + y_lo), z: 4, core: 2. Of those that a mesh axis runs over, the one named last changes fastest.
Arguments:
- records: bfloat16 [16, 3, 8192], P('sta', None, 'tm'), may hold values from -6 to 6
- templates: bfloat16 [128, 16, 3, 200], P('tm', 'sta'), may hold values from -0.25 to 0.25
- moveouts: int32 [128, 16], P(None, 'sta'), may hold values from 0 to 184, as said below
Outputs:
- detection: float32 [128, 8192], P('sta', 'tm')
The draws below stay inside these ranges and needn't reach their ends.
Inputs may be any that keep to these rules, and one draw needn't show every extreme that they name: `moveouts`: for every template, some station has moveout 0 and some station has moveout 184.
All inputs are finite; a program needn't handle non-finite values.
Results may differ from the reference program's by a relative error of at most 0.0003.
Values may be sent and summed in bfloat16 or wider, within the bound.
No kernel may reach another device: no remote copies, remote signals or barrier semaphores. Data moves between devices by JAX's collectives and lax.ppermute only.
A program may use at most 64 MiB of HBM per device.

```python
import jax
import jax.numpy as jnp
from jax import lax

K = 128
L = 200
M_MAX = 184
HALO = 384
STATIONS = 16
TIMES = 8192


def draw_moveouts(key, part):
    first, second, third = jax.random.split(key, 3)
    values = jax.random.randint(first, (K, STATIONS), 0, M_MAX + 1)
    highest = jax.random.randint(second, (K,), 0, STATIONS)
    lowest = (highest + 1 + jax.random.randint(third, (K,), 0, STATIONS - 1)) % STATIONS
    columns = jnp.arange(STATIONS)[None, :]
    values = jnp.where(columns == highest[:, None], M_MAX, values)
    values = jnp.where(columns == lowest[:, None], 0, values)
    return values.astype(jnp.int32)


def block_levels(rng, shape, pieces, least, top_value):
    def one(axis_at, parts):
        steps = jax.random.uniform(jax.random.fold_in(jax.random.fold_in(rng, 6), axis_at), (parts,), jnp.float32, least / len(pieces), top_value / len(pieces))
        return jnp.repeat(jnp.exp(steps), shape[axis_at] // parts).reshape((-1,) + (1,) * (len(shape) - axis_at - 1))

    level = one(*pieces[0])
    for cut in pieces[1:]:
        level = level * one(*cut)
    return level


def normal_values(rng, shape, spread, bound, cuts=(), dtype=jnp.bfloat16):
    gain = block_levels(rng, shape, cuts, -0.22, 0.18) if cuts else 1.0
    array = jax.random.normal(rng, shape, jnp.float32) * spread * gain
    return jnp.minimum(jnp.maximum(array, -bound), bound).astype(dtype)


def setup_inputs(seed: int = 0) -> dict:
    seeds = jax.random.split(jax.random.key(seed), 4)
    return {
        "records": normal_values(seeds[0], (STATIONS, 3, TIMES), 1.0, 6.0, ((0, 8), (2, 16))),
        "templates": normal_values(seeds[1], (K, STATIONS, 3, L), (3 * L) ** -0.5, 0.25, ((0, 16), (1, 8))),
        "moveouts": draw_moveouts(jax.random.fold_in(seeds[3], 71), 0),
    }


EPS = 1e-06

def energy_inverse(extended, length):
    wide = extended.astype(jnp.float32)
    squares = lax.optimization_barrier(jnp.sum(wide * wide, axis=1))
    energy = lax.reduce_window(squares, jnp.float32(0.0), lax.add, (1, length), (1, 1), 'VALID')
    return lax.rsqrt(energy + EPS)

def window_at(series, offset, extent):
    return lax.dynamic_slice_in_dim(series, offset, extent, 0)

def correlate(extended, inverse, waveforms, shifts, extent):
    stations = extended.shape[0]
    members = waveforms.shape[0]
    length = waveforms.shape[3]
    inputs = extended.astype(jnp.float32).reshape(1, stations * 3, extended.shape[2])
    kernel = jnp.transpose(waveforms.astype(jnp.float32), (1, 0, 2, 3)).reshape(stations * members, 3, length)
    correlations = lax.conv_general_dilated(inputs, kernel, (1,), 'VALID', dimension_numbers=('NCH', 'OIH', 'NCH'), feature_group_count=stations, precision=lax.Precision.HIGHEST)
    scaled = correlations.reshape(stations, members, -1) * inverse[:, None, :]
    offsets = jnp.transpose(shifts).astype(jnp.int32)
    picked = jax.vmap(jax.vmap(lambda series, offset: window_at(series, offset, extent)))(scaled, offsets)
    return lax.optimization_barrier(jnp.sum(picked, axis=0))

def reference(records, templates, moveouts):
    stations = records.shape[0]
    extent = records.shape[2]
    padded = jnp.pad(records, ((0, 0), (0, 0), (0, HALO)))
    inverse = energy_inverse(padded, L)
    groups = templates.reshape(K // 8, 8, stations, 3, L)
    shifts = moveouts.reshape(K // 8, 8, stations)

    def single(pair):
        return correlate(padded, inverse, pair[0], pair[1], extent)
    result = lax.map(single, (groups, shifts))
    return result.reshape(K, extent)
```

```python
import jax
import jax.numpy as jnp
from jax import lax
from jax.experimental import pallas as pl
from jax.experimental.pallas import tpu as pltpu
from jax.sharding import PartitionSpec as P

HALO = 384
EPS = 1e-06
LENGTH = 200
LAG = 64
REACH = 768
SPAN = 896
WIDE = 1024
ROWS = 8
PARTS = LENGTH // LAG + 1


def coordinates(time_index, station_index):
    return time_index // 4, (time_index // 2) % 2, time_index % 2, station_index // 4, station_index % 4


def transposition():
    pairs = []
    for i in range(16):
        for j in range(8):
            x, y, core, high, z = coordinates(i, j)
            target = i // 2
            near, level = target // 4, target % 4
            there = ((x + z - level) % 4) * 4 + (y ^ high ^ near) * 2 + core
            pairs.append((i * 8 + j, there * 8 + target))
    return pairs


def permuted(value, axis, size, move):
    return lax.ppermute(value, axis, [(source, move(source)) for source in range(size)])


def take(value, index):
    return jnp.take_along_axis(value, index, axis=1)


def windows(series, width, steps):
    lane = lax.broadcasted_iota(jnp.int32, (steps.shape[0], 128), 1) + steps
    index, stays = lane & 127, lane < 128
    picked = [take(series[:, at : at + 128], index) for at in range(0, width + 128, 128)]
    return jnp.concatenate([jnp.where(stays, a, b) for a, b in zip(picked[:-1], picked[1:])], axis=1)


def ahead(value, steps):
    return pltpu.roll(value, value.shape[1] - steps, 1)


def kernel(templates_ref, records_ref, out_ref, scale_ref, lagged_ref):
    i, j = lax.axis_index("tm"), lax.axis_index("sta")
    lags = lax.broadcasted_iota(jnp.int32, (LAG, 128), 0)
    energies = []
    for slot in range(8):
        wide = records_ref[slot].astype(jnp.float32)
        squares = wide * wide
        energies.append(squares[0:2] + squares[2:4] + squares[4:6])
        padded = jnp.concatenate([wide, jnp.zeros((ROWS, WIDE - SPAN), jnp.float32)], axis=1)
        for station in range(2):
            for c in range(3):
                row = jnp.broadcast_to(padded[c * 2 + station : c * 2 + station + 1], (LAG, WIDE))
                lagged_ref[slot * 2 + station, c * LAG : (c + 1) * LAG] = windows(row, SPAN, lags).astype(jnp.bfloat16)
    energy = jnp.concatenate(energies, axis=0)
    two = energy + ahead(energy, 1)
    four = two + ahead(two, 2)
    eight = four + ahead(four, 4)
    total, steps = eight, 8
    while steps < 128:
        if steps == 64:
            sixty = total
        total, steps = total + ahead(total, steps), steps * 2
    total = total + ahead(sixty, 128) + ahead(eight, 192)
    scale = lax.rsqrt(total[:, :REACH] + EPS)
    for row in range(16):
        scale_ref[row] = jnp.broadcast_to(scale[row : row + 1], (ROWS, REACH))

    x, y, _, _, z = coordinates(i, j)
    result = jnp.zeros((16, 512), jnp.float32)
    for dx in range(4):
        for dy in range(2):
            slot = lax.rem(x + dx - j // 2 + 8, 4) * 2 + lax.rem(y + dy + j, 2)
            for station in range(2):
                blocks = [templates_ref[dx, dy, core].astype(jnp.float32) for core in range(2)]
                rows = []
                for a in range(PARTS):
                    for block in blocks:
                        pieces = []
                        for c in range(3):
                            top = (station * 3 + c) * ROWS
                            piece = block[top : top + ROWS, a * LAG : (a + 1) * LAG]
                            if (a + 1) * LAG > LENGTH:
                                inside = lax.broadcasted_iota(jnp.int32, (ROWS, LAG), 1) < LENGTH - a * LAG
                                piece = jnp.where(inside, piece, 0.0)
                            pieces.append(piece)
                        rows.append(jnp.concatenate(pieces, axis=1))
                left = jnp.concatenate(rows, axis=0).astype(jnp.bfloat16)
                right = lagged_ref[slot * 2 + station]
                sums = jnp.dot(left, right, preferred_element_type=jnp.float32)
                even = sums[0:16, 0:REACH] + sums[32:48, 128 : 128 + REACH]
                odd = sums[16:32, 0:REACH] + sums[48:64, 128 : 128 + REACH]
                values = even + ahead(odd, LAG)
                values = values * jnp.concatenate([scale_ref[slot * 2 + station]] * 2, axis=0)
                top = station * 3 * ROWS
                moves = jnp.concatenate([block[top : top + ROWS, LENGTH : LENGTH + 1] for block in blocks], axis=0)
                moves = jnp.broadcast_to(moves, (16, 128)).astype(jnp.int32)
                far = moves >= 128
                lane = lax.broadcasted_iota(jnp.int32, (16, 128), 1) + (moves & 127)
                index, stays = lane & 127, lane < 128
                picked = [take(values[:, at : at + 128], index) for at in range(0, REACH, 128)]
                picked = [jnp.where(far, b, a) for a, b in zip(picked[:-1], picked[1:])]
                result += jnp.concatenate([jnp.where(stays, a, b) for a, b in zip(picked[:-1], picked[1:])], axis=1)
    swapped = lax.rem(i, 2) == 1
    low, high = result[0:8], result[8:16]
    out_ref[0:8] = jnp.where(swapped, high, low)
    out_ref[8:16] = jnp.where(swapped, low, high)


def local(records, templates, moveouts):
    i = lax.axis_index("tm")
    mine = lax.dynamic_slice_in_dim(moveouts, i * ROWS, ROWS, 0).astype(jnp.bfloat16)
    mine = jnp.broadcast_to(jnp.transpose(mine)[:, None, :, None], (2, 3, ROWS, 256 - LENGTH))
    packet = jnp.concatenate([jnp.transpose(templates, (1, 2, 0, 3)), mine], axis=3).reshape(6 * ROWS, 256)
    packet = lax.ppermute(packet, ("tm", "sta"), transposition())

    following = lax.ppermute(records[:, :, :HALO], "tm", [(s, s - 1) for s in range(1, 16)])
    extended = jnp.transpose(jnp.concatenate([records, following], axis=2), (1, 0, 2)).reshape(6, SPAN)
    extended = jnp.concatenate([extended, jnp.zeros((2, SPAN), jnp.bfloat16)], axis=0)

    packet = jnp.stack([packet, permuted(packet, "tm", 16, lambda s: s ^ 2)])
    extended = jnp.stack([extended, permuted(extended, "sta", 8, lambda s: s ^ 4)])
    packet = jnp.stack([packet] + [permuted(packet, "tm", 16, lambda s, d=d: (s + 16 - 4 * d) % 16) for d in (1, 2, 3)])
    extended = jnp.stack(
        [extended] + [permuted(extended, "sta", 8, lambda s, d=d: s // 4 * 4 + (s + 4 - d) % 4) for d in (1, 2, 3)]
    )
    packet = jnp.stack([packet, permuted(packet, "tm", 16, lambda s: s ^ 1)], axis=2)

    return pl.pallas_call(
        kernel,
        out_shape=jax.ShapeDtypeStruct((16, 512), jnp.float32),
        in_specs=[pl.BlockSpec(memory_space=pltpu.VMEM)] * 2,
        out_specs=pl.BlockSpec(memory_space=pltpu.VMEM),
        scratch_shapes=[
            pltpu.VMEM((16, ROWS, REACH), jnp.float32),
            pltpu.VMEM((16, 3 * LAG, SPAN), jnp.bfloat16),
        ],
        compiler_params=pltpu.CompilerParams(vmem_limit_bytes=40 * 1024 * 1024),
        cost_estimate=pl.CostEstimate(flops=2 * 128 * 2 * 600 * 696, bytes_accessed=600_000, transcendentals=0),
    )(packet, extended.reshape(8, ROWS, SPAN))


def solution(mesh):
    return jax.shard_map(
        local,
        mesh=mesh,
        in_specs=(P("sta", None, "tm"), P("tm", "sta", None, None), P(None, "sta")),
        out_specs=P("sta", "tm"),
        check_vma=False,
    )
```

```python
import jax
import jax.numpy as jnp
from jax import lax
from jax.experimental import pallas as pl
from jax.experimental.pallas import tpu as pltpu
from jax.sharding import PartitionSpec as P

EPS = 1e-06
LENGTH = 200
LAG = 64
REACH = 768
SPAN = 896
BLOCK = 6 * 8
WIDE = 1024
ROWS = 8
SENDER = 1
PARTS = LENGTH // LAG + 1


def coordinates(time_index, station_index):
    return time_index // 4, (time_index // 2) % 2, time_index % 2, station_index // 4, station_index % 4


def exchange(value, templates_to, records_to):
    pairs = []
    for i in range(16):
        for j in range(8):
            target = (templates_to if i % 2 == SENDER else records_to)(*coordinates(i, j))
            if target is not None:
                x, y, core, high, z = target
                pairs.append((i * 8 + j, ((x * 2 + y) * 2 + core) * 8 + high * 4 + z))
    return lax.ppermute(value, ("tm", "sta"), pairs)


def other_core(x, y, core, high, z):
    return x, y, 1 - core, high, z


def to_owner(x, y, core, high, z):
    near, level = x // 2, x % 2 * 2 + y
    return (x + 2 + z - level) % 4, y ^ high ^ near, core, near, level


def to_previous(x, y, core, high, z):
    return None if x + y == 0 else (x - 1 + y, 1 - y, core, high, z)


def across_y(x, y, core, high, z):
    return x, 1 - y, core, high, z


def across_high(x, y, core, high, z):
    return x, y, core, 1 - high, z


def back_x(steps):
    return lambda x, y, core, high, z: ((x - steps) % 4, y, core, high, z)


def back_z(steps):
    return lambda x, y, core, high, z: (x, y, core, high, (z - steps) % 4)


def take(value, index):
    return jnp.take_along_axis(value, index, axis=1)


def windows(series):
    return pltpu.roll(series, WIDE - LAG + 1, 1, stride=1, stride_axis=0)[:, :SPAN].astype(jnp.bfloat16)


def ahead(value, steps):
    return pltpu.roll(value, value.shape[1] - steps, 1)


def kernel(gathered_ref, out_ref, scale_ref, lagged_ref, flipped_ref, moves_ref):
    i, j = lax.axis_index("tm"), lax.axis_index("sta")
    x, y, core, _, z = coordinates(i, j)
    sender = jnp.where(core == SENDER, 0, 1)
    energies = []
    for slot in range(8):
        rows = pl.ds(pl.multiple_of(core * 16, 16), 32)
        chunks = gathered_ref[1 - sender, slot // 2, slot % 2, 0, rows].astype(jnp.float32)
        wide = jnp.concatenate([chunks[at * ROWS : (at + 1) * ROWS] for at in range(4)], axis=1)
        squares = wide * wide
        energies.append(squares[0:2] + squares[2:4] + squares[4:6])
        for station in range(2):
            for c in range(3):
                row = jnp.broadcast_to(wide[c * 2 + station : c * 2 + station + 1], (LAG, WIDE))
                lagged_ref[slot * 2 + station, c * LAG : (c + 1) * LAG] = windows(row)
    energy = jnp.concatenate(energies, axis=0)
    two = energy + ahead(energy, 1)
    four = two + ahead(two, 2)
    eight = four + ahead(four, 4)
    total, steps = eight, 8
    while steps < 128:
        if steps == 64:
            sixty = total
        total, steps = total + ahead(total, steps), steps * 2
    total = total + ahead(sixty, 128) + ahead(eight, 192)
    scale = lax.rsqrt(total[:, :REACH] + EPS)
    for row in range(16):
        scale_ref[row] = jnp.broadcast_to(scale[row : row + 1], (ROWS, REACH))

    blocks = gathered_ref[sender].reshape(16 * BLOCK, 256)
    source = lax.broadcasted_iota(jnp.int32, (256, 256), 0)
    target = lax.broadcasted_iota(jnp.int32, (256, 256), 1)
    flip = jnp.where((source < LENGTH) & (source == (target ^ (LAG - 1))), 1.0, 0.0).astype(jnp.bfloat16)
    flipped_ref[...] = jnp.dot(blocks, flip, preferred_element_type=jnp.float32)
    spread = jnp.where(source[:, :128] == LENGTH, 1.0, 0.0).astype(jnp.bfloat16)
    moves_ref[...] = jnp.dot(blocks, spread, preferred_element_type=jnp.float32).astype(jnp.int32)

    lane = lax.broadcasted_iota(jnp.int32, (16, 128), 1)
    result = jnp.zeros((16, 512), jnp.float32)
    for dx in range(4):
        for dy in range(2):
            slot = lax.rem(x + dx - j // 2 + 6, 4) * 2 + lax.rem(y + dy + j, 2)
            for station in range(2):
                tops = [((dx * 2 + dy) * 2 + half) * BLOCK + station * 3 * ROWS for half in range(2)]
                rows = []
                for a in range(PARTS):
                    for top in tops:
                        pieces = [
                            flipped_ref[top + c * ROWS : top + (c + 1) * ROWS, a * LAG : (a + 1) * LAG] for c in range(3)
                        ]
                        rows.append(jnp.concatenate(pieces, axis=1))
                left = jnp.concatenate(rows, axis=0).astype(jnp.bfloat16)
                right = lagged_ref[slot * 2 + station]
                sums = jnp.dot(left, right, preferred_element_type=jnp.float32)
                even = sums[0:16, 0:REACH] + sums[32:48, 128 : 128 + REACH]
                odd = sums[16:32, 0:REACH] + sums[48:64, 128 : 128 + REACH]
                values = even + ahead(odd, LAG)
                values = values * jnp.concatenate([scale_ref[slot * 2 + station]] * 2, axis=0)
                moves = jnp.concatenate([moves_ref[top : top + ROWS] for top in tops], axis=0)
                near = moves & 127
                picked = [values[:, at : at + 128] for at in range(0, REACH, 128)]
                picked = [jnp.where(moves >= 128, b, a) for a, b in zip(picked[:-1], picked[1:])]
                picked = [jnp.where(lane < near, b, a) for a, b in zip(picked[:-1], picked[1:])]
                index = (lane + near) & 127
                result += jnp.concatenate([take(value, index) for value in picked], axis=1)
    out_ref[...] = result


def local(records, templates, moveouts):
    i = lax.axis_index("tm")
    mine = lax.dynamic_slice_in_dim(moveouts, i * ROWS, ROWS, 0).astype(jnp.bfloat16)
    mine = jnp.broadcast_to(jnp.transpose(mine)[:, None, :, None], (2, 3, ROWS, 256 - LENGTH))
    packet = jnp.concatenate([jnp.transpose(templates, (1, 2, 0, 3)), mine], axis=3).reshape(6 * ROWS, 256)
    series = jnp.transpose(records, (1, 0, 2)).reshape(6, 512)
    series = jnp.concatenate([series, jnp.zeros((2, 512), jnp.bfloat16)], axis=0)
    series = jnp.concatenate([series[:, :256], series[:, 256:]], axis=0)

    first = i % 2 == SENDER
    spare = jnp.zeros((BLOCK, 256), jnp.bfloat16)
    series = jnp.concatenate([series, spare[16:]], axis=0)
    came = exchange(jnp.where(first, series, packet), other_core, other_core)
    mine = jnp.where(first, packet, series)
    next_came = exchange(jnp.concatenate([jnp.where(first, came, mine), mine], axis=0), to_owner, to_previous)
    chip_series = jnp.concatenate([mine[:16], came[:16], next_came[:16], spare], axis=0)
    held = jnp.where(first, next_came, chip_series)
    held = jnp.stack([held, exchange(held, across_y, across_high)])
    held = jnp.stack([held] + [exchange(held, back_x(steps), back_z(steps)) for steps in (1, 2, 3)])
    held = jnp.stack([held, exchange(held, other_core, other_core)])

    return pl.pallas_call(
        kernel,
        out_shape=jax.ShapeDtypeStruct((16, 512), jnp.float32),
        in_specs=[pl.BlockSpec(memory_space=pltpu.VMEM)],
        out_specs=pl.BlockSpec(memory_space=pltpu.VMEM),
        scratch_shapes=[
            pltpu.VMEM((16, ROWS, REACH), jnp.float32),
            pltpu.VMEM((16, 3 * LAG, SPAN), jnp.bfloat16),
            pltpu.VMEM((16 * BLOCK, 256), jnp.float32),
            pltpu.VMEM((16 * BLOCK, 128), jnp.int32),
        ],
        compiler_params=pltpu.CompilerParams(vmem_limit_bytes=40 * 1024 * 1024),
        cost_estimate=pl.CostEstimate(flops=2 * 128 * 2 * 600 * 696, bytes_accessed=600_000, transcendentals=0),
    )(held.reshape(2, 4, 2, 2, BLOCK, 256))


def solution(mesh):
    return jax.shard_map(
        local,
        mesh=mesh,
        in_specs=(P("sta", None, "tm"), P("tm", "sta", None, None), P(None, "sta")),
        out_specs=P("sta", "tm"),
        check_vma=False,
    )
```

```python
import jax
import jax.numpy as jnp
from jax import lax
from jax.experimental import pallas as pl
from jax.experimental.pallas import tpu as pltpu
from jax.sharding import PartitionSpec as P

EPS = 1e-06
LENGTH = 200
LAG = 64
REACH = 768
SPAN = 896
TAPS = 640
WIDE = 1024
ROWS = 8
SENDER = 1
PARTS = LENGTH // LAG + 1
GROUP = 128 // LAG
COLUMNS = 128 if 3 * LAG <= 128 else 256


def coordinates(time_index, station_index):
    return time_index // 4, (time_index // 2) % 2, time_index % 2, station_index // 4, station_index % 4


def exchange(value, templates_to, records_to):
    pairs = []
    for i in range(16):
        for j in range(8):
            target = (templates_to if i % 2 == SENDER else records_to)(*coordinates(i, j))
            x, y, core, high, z = target
            pairs.append((i * 8 + j, ((x * 2 + y) * 2 + core) * 8 + high * 4 + z))
    return lax.ppermute(value, ("tm", "sta"), pairs)


def other_core(x, y, core, high, z):
    return x, y, 1 - core, high, z


def to_owner(x, y, core, high, z):
    near, level = x // 2, x % 2 * 2 + y
    return (x + 2 + z - level) % 4, y ^ high ^ near, core, near, level


def to_previous(x, y, core, high, z):
    return (x - 1 + y) % 4, 1 - y, core, high, z


def to_owner_across(x, y, core, high, z):
    x, y, core, high, z = to_owner(x, y, core, high, z)
    return x, 1 - y, core, high, z


def to_previous_across(x, y, core, high, z):
    x, y, core, high, z = to_previous(x, y, core, high, z)
    return x, y, core, 1 - high, z


def across_y(x, y, core, high, z):
    return x, 1 - y, core, high, z


def across_high(x, y, core, high, z):
    return x, y, core, 1 - high, z


def back_x(steps):
    return lambda x, y, core, high, z: ((x - steps) % 4, y, core, high, z)


def back_z(steps):
    return lambda x, y, core, high, z: (x, y, core, high, (z - steps) % 4)


def take(value, index):
    return jnp.take_along_axis(value, index, axis=1)


def windows(series):
    return pltpu.roll(series, WIDE - LAG + 1, 1, stride=1, stride_axis=0)[:, :SPAN].astype(jnp.bfloat16)


def ahead(value, steps):
    return pltpu.roll(value, value.shape[1] - steps, 1)


def arrangement():
    source = lax.broadcasted_iota(jnp.int32, (TAPS, PARTS * COLUMNS), 0)
    column = lax.broadcasted_iota(jnp.int32, (TAPS, PARTS * COLUMNS), 1)
    place = column % COLUMNS
    lag = column // COLUMNS * LAG + LAG - 1 - place % LAG
    wanted = place // LAG * LENGTH + lag
    return jnp.where((source == wanted) & (lag < LENGTH) & (place < 3 * LAG), 1.0, 0.0).astype(jnp.bfloat16)


def kernel(gathered_ref, arrangement_ref, out_ref, scale_ref, lagged_ref, left_ref, moves_ref, chosen_ref, values_ref):
    i, j = lax.axis_index("tm"), lax.axis_index("sta")
    x, y, core, _, z = coordinates(i, j)
    sender = jnp.where(core == SENDER, 0, 1)
    template = lax.broadcasted_iota(jnp.int32, (16, 128), 0)
    lane = lax.broadcasted_iota(jnp.int32, (16, 128), 1)
    own = lane == template + 16 * j
    energies = []
    for slot in range(8):
        held = gathered_ref[1 - sender, slot // 2, slot % 2].astype(jnp.float32)
        pieces = [held[at : at + ROWS, :512] for at in (0, 8, 16)]
        wide = jnp.concatenate([jnp.where(core == 0, a, b) for a, b in zip(pieces[:-1], pieces[1:])], axis=1)
        squares = wide * wide
        energies.append(squares[0:2] + squares[2:4] + squares[4:6])
        for station in range(2):
            at = slot * 2 + station
            shifts = jnp.broadcast_to(held[24 + station : 25 + station, :128], (16, 128))
            chosen_ref[at * 16 : (at + 1) * 16] = jnp.where(own, shifts, 0.0).astype(jnp.bfloat16)
            for c in range(3):
                row = jnp.broadcast_to(wide[c * 2 + station : c * 2 + station + 1], (LAG, WIDE))
                lagged_ref[at, c * LAG : (c + 1) * LAG] = windows(row)
    energy = jnp.concatenate(energies, axis=0)
    four = energy + ahead(energy, 1) + (ahead(energy, 2) + ahead(energy, 3))
    eight = four + ahead(four, 4)
    sixteen = eight + (ahead(four, 8) + ahead(four, 12))
    sixty = sixteen + ahead(sixteen, 16) + (ahead(sixteen, 32) + ahead(sixteen, 48))
    total = sixty + ahead(sixty, 64) + (ahead(sixty, 128) + ahead(eight, 192))
    scale = lax.rsqrt(total[:, :REACH] + EPS)
    for row in range(16):
        scale_ref[row] = jnp.broadcast_to(scale[row : row + 1], (ROWS, REACH))

    moves_ref[...] = jnp.dot(
        chosen_ref[...], jnp.ones((128, 128), jnp.bfloat16), preferred_element_type=jnp.float32
    ).astype(jnp.int32)
    blocks = gathered_ref[sender].reshape(256, TAPS)
    left_ref[...] = jnp.dot(blocks, arrangement_ref[...], preferred_element_type=jnp.float32).astype(jnp.bfloat16)

    result = jnp.zeros((16, 512), jnp.float32)
    for dx in range(4):
        for dy in range(2):
            slot = lax.rem(x + dx - j // 2 + 6, 4) * 2 + lax.rem(y + dy + j, 2)
            for station in range(2):
                top = (dx * 2 + dy) * 32 + station * 16
                left = jnp.concatenate(
                    [left_ref[top : top + 16, a * COLUMNS : a * COLUMNS + 3 * LAG] for a in range(PARTS)], axis=0
                )
                at = slot * 2 + station
                sums = jnp.dot(left, lagged_ref[at], preferred_element_type=jnp.float32)
                parts = [sums[a * 16 : (a + 1) * 16] for a in range(PARTS)]
                values = None
                for group in range(GROUP - 1, -1, -1):
                    term = parts[group]
                    if group + GROUP < PARTS:
                        term = term[:, :REACH] + parts[group + GROUP][:, 128:]
                    values = term if values is None else term + ahead(values, LAG)[:, :REACH]
                values = values * jnp.concatenate([scale_ref[at]] * 2, axis=0)
                values_ref[(dx * 2 + dy) * 2 + station] = values
    for dx in range(4):
        for dy in range(2):
            slot = lax.rem(x + dx - j // 2 + 6, 4) * 2 + lax.rem(y + dy + j, 2)
            for station in range(2):
                values = values_ref[(dx * 2 + dy) * 2 + station]
                at = slot * 2 + station
                moves = moves_ref[pl.ds(pl.multiple_of(at * 16, 16), 16)]
                near = moves & 127
                picked = [values[:, at : at + 128] for at in range(0, REACH, 128)]
                picked = [jnp.where(moves >= 128, b, a) for a, b in zip(picked[:-1], picked[1:])]
                picked = [jnp.where(lane < near, b, a) for a, b in zip(picked[:-1], picked[1:])]
                index = (lane + near) & 127
                result += jnp.concatenate([take(value, index) for value in picked], axis=1)
    out_ref[...] = result


def bring(*refs):
    half = len(refs) // 2
    for source, target in zip(refs[:half], refs[half:]):
        target[...] = source[...]


def brought(*values):
    return pl.pallas_call(
        bring,
        out_shape=[pltpu.VMEM(value.shape, value.dtype) for value in values],
        in_specs=[pl.BlockSpec(memory_space=pltpu.VMEM)] * len(values),
        out_specs=[pl.BlockSpec(memory_space=pltpu.VMEM)] * len(values),
    )(*values)


def local(records, templates, moveouts):
    i = lax.axis_index("tm")
    first = i % 2 == SENDER
    records, templates, moveouts = brought(
        jnp.transpose(records, (1, 0, 2)), jnp.transpose(templates, (0, 2, 1, 3)), jnp.transpose(moveouts)
    )
    packet = jnp.pad(jnp.transpose(templates, (2, 0, 1, 3)).reshape(16, 3 * LENGTH), ((0, 0), (0, TAPS - 3 * LENGTH)))
    series = jnp.pad(records.reshape(6, 512), ((0, 2), (0, TAPS - 512)))
    shifts = jnp.pad(moveouts.astype(jnp.bfloat16), ((0, 6), (0, TAPS - 128)))
    series = jnp.concatenate([series, shifts], axis=0)
    came = exchange(jnp.where(first, series, packet), other_core, other_core)
    mine = jnp.where(first, packet, series)
    held = jnp.concatenate([came[:8], mine[:8], came[8:], mine[8:]], axis=0)
    one = exchange(held, to_owner, to_previous)
    two = exchange(held, to_owner_across, across_high)
    three = exchange(held, across_y, to_previous_across)
    order = arrangement()
    ends = i // 2 == 7
    near_after = jnp.where(ends, jnp.zeros_like(one[8:16]), one[8:16])
    far_after = jnp.where(ends, jnp.zeros_like(three[8:16]), three[8:16])
    near = jnp.where(first, one, jnp.concatenate([mine[:8], came[:8], near_after, mine[8:]], axis=0))
    far = jnp.where(first, two, jnp.concatenate([two[8:16], two[:8], far_after, two[24:]], axis=0))
    held = jnp.stack([near, far])
    held = jnp.stack([held] + [exchange(held, back_x(steps), back_z(steps)) for steps in (1, 2, 3)])
    held = jnp.stack([held, exchange(held, other_core, other_core)])

    return pl.pallas_call(
        kernel,
        out_shape=jax.ShapeDtypeStruct((16, 512), jnp.float32),
        in_specs=[pl.BlockSpec(memory_space=pltpu.VMEM)] * 2,
        out_specs=pl.BlockSpec(memory_space=pltpu.VMEM),
        scratch_shapes=[
            pltpu.VMEM((16, ROWS, REACH), jnp.float32),
            pltpu.VMEM((16, 3 * LAG, SPAN), jnp.bfloat16),
            pltpu.VMEM((256, PARTS * COLUMNS), jnp.bfloat16),
            pltpu.VMEM((256, 128), jnp.int32),
            pltpu.VMEM((256, 128), jnp.bfloat16),
            pltpu.VMEM((16, 16, REACH), jnp.float32),
        ],
        compiler_params=pltpu.CompilerParams(vmem_limit_bytes=40 * 1024 * 1024),
        cost_estimate=pl.CostEstimate(flops=2 * 128 * 2 * 600 * 696, bytes_accessed=600_000, transcendentals=0),
    )(held, order)


def solution(mesh):
    return jax.shard_map(
        local,
        mesh=mesh,
        in_specs=(P("sta", None, "tm"), P("tm", "sta", None, None), P(None, "sta")),
        out_specs=P("sta", "tm"),
        check_vma=False,
    )
```

```python
import jax
import jax.numpy as jnp
from jax import lax
from jax.experimental import pallas as pl
from jax.experimental.pallas import tpu as pltpu
from jax.sharding import PartitionSpec as P

EPS = 1e-06
LENGTH = 200
LAG = 64
REACH = 768
SPAN = 896
TAPS = 640
WIDE = 1024
ROWS = 8
SENDER = 1
PARTS = LENGTH // LAG + 1
GROUP = 128 // LAG
COLUMNS = 128 if 3 * LAG <= 128 else 256


def coordinates(time_index, station_index):
    return time_index // 4, (time_index // 2) % 2, time_index % 2, station_index // 4, station_index % 4


def exchange(value, templates_to, records_to):
    pairs = []
    for i in range(16):
        for j in range(8):
            target = (templates_to if i % 2 == SENDER else records_to)(*coordinates(i, j))
            x, y, core, high, z = target
            pairs.append((i * 8 + j, ((x * 2 + y) * 2 + core) * 8 + high * 4 + z))
    return lax.ppermute(value, ("tm", "sta"), pairs)


def other_core(x, y, core, high, z):
    return x, y, 1 - core, high, z


def to_owner(x, y, core, high, z):
    near, level = x // 2, x % 2 * 2 + y
    return (x + 2 + z - level) % 4, y ^ high ^ near, core, near, level


def to_previous(x, y, core, high, z):
    return (x - 1 + y) % 4, 1 - y, core, high, z


def to_owner_across(x, y, core, high, z):
    x, y, core, high, z = to_owner(x, y, core, high, z)
    return x, 1 - y, core, high, z


def to_previous_across(x, y, core, high, z):
    x, y, core, high, z = to_previous(x, y, core, high, z)
    return x, y, core, 1 - high, z


def across_y(x, y, core, high, z):
    return x, 1 - y, core, high, z


def across_high(x, y, core, high, z):
    return x, y, core, 1 - high, z


def back_x(steps):
    return lambda x, y, core, high, z: ((x - steps) % 4, y, core, high, z)


def back_z(steps):
    return lambda x, y, core, high, z: (x, y, core, high, (z - steps) % 4)


def take(value, index):
    return jnp.take_along_axis(value, index, axis=1)


def windows(series):
    return pltpu.roll(series, WIDE - LAG + 1, 1, stride=1, stride_axis=0)[:, :SPAN].astype(jnp.bfloat16)


def ahead(value, steps):
    return pltpu.roll(value, value.shape[1] - steps, 1)


def arrangement():
    source = lax.broadcasted_iota(jnp.int32, (TAPS, PARTS * COLUMNS), 0)
    column = lax.broadcasted_iota(jnp.int32, (TAPS, PARTS * COLUMNS), 1)
    place = column % COLUMNS
    lag = column // COLUMNS * LAG + LAG - 1 - place % LAG
    wanted = place // LAG * LENGTH + lag
    return jnp.where((source == wanted) & (lag < LENGTH) & (place < 3 * LAG), 1.0, 0.0).astype(jnp.bfloat16)


def kernel(gathered_ref, arrangement_ref, out_ref, scale_ref, lagged_ref, left_ref, moves_ref, chosen_ref, values_ref):
    i, j = lax.axis_index("tm"), lax.axis_index("sta")
    x, y, core, _, z = coordinates(i, j)
    sender = jnp.where(core == SENDER, 0, 1)
    template = lax.broadcasted_iota(jnp.int32, (16, 128), 0)
    lane = lax.broadcasted_iota(jnp.int32, (16, 128), 1)
    own = lane == template + 16 * j
    energies = []
    for slot in range(8):
        level = lax.rem(x + slot // 2 - j // 2 + 6, 4)
        half = lax.rem(y + slot % 2 + j, 2)
        held = gathered_ref[1 - sender, level, half].astype(jnp.float32)
        pieces = [held[at : at + ROWS, :512] for at in (0, 8, 16)]
        wide = jnp.concatenate([jnp.where(core == 0, a, b) for a, b in zip(pieces[:-1], pieces[1:])], axis=1)
        squares = wide * wide
        energies.append(squares[0:2] + squares[2:4] + squares[4:6])
        for station in range(2):
            at = slot * 2 + station
            shifts = jnp.broadcast_to(held[24 + station : 25 + station, :128], (16, 128))
            chosen_ref[at * 16 : (at + 1) * 16] = jnp.where(own, shifts, 0.0).astype(jnp.bfloat16)
            for c in range(3):
                row = jnp.broadcast_to(wide[c * 2 + station : c * 2 + station + 1], (LAG, WIDE))
                lagged_ref[at, c * LAG : (c + 1) * LAG] = windows(row)
    energy = jnp.concatenate(energies, axis=0)
    four = energy + ahead(energy, 1) + (ahead(energy, 2) + ahead(energy, 3))
    eight = four + ahead(four, 4)
    sixteen = eight + (ahead(four, 8) + ahead(four, 12))
    sixty = sixteen + ahead(sixteen, 16) + (ahead(sixteen, 32) + ahead(sixteen, 48))
    total = sixty + ahead(sixty, 64) + (ahead(sixty, 128) + ahead(eight, 192))
    scale = lax.rsqrt(total[:, :REACH] + EPS)
    for row in range(16):
        scale_ref[row] = jnp.broadcast_to(scale[row : row + 1], (ROWS, REACH))

    moves_ref[...] = jnp.dot(
        chosen_ref[...], jnp.ones((128, 128), jnp.bfloat16), preferred_element_type=jnp.float32
    ).astype(jnp.int32)
    blocks = gathered_ref[sender].reshape(256, TAPS)
    left_ref[...] = jnp.dot(blocks, arrangement_ref[...], preferred_element_type=jnp.float32).astype(jnp.bfloat16)

    result = jnp.zeros((16, 512), jnp.float32)
    for dx in range(4):
        for dy in range(2):
            for station in range(2):
                at = (dx * 2 + dy) * 2 + station
                top = at * 16
                left = jnp.concatenate(
                    [left_ref[top : top + 16, a * COLUMNS : a * COLUMNS + 3 * LAG] for a in range(PARTS)], axis=0
                )
                sums = jnp.dot(left, lagged_ref[at], preferred_element_type=jnp.float32)
                parts = [sums[a * 16 : (a + 1) * 16] for a in range(PARTS)]
                values = None
                for group in range(GROUP - 1, -1, -1):
                    term = parts[group]
                    if group + GROUP < PARTS:
                        term = term[:, :REACH] + parts[group + GROUP][:, 128:]
                    values = term if values is None else term + ahead(values, LAG)[:, :REACH]
                values = values * jnp.concatenate([scale_ref[at]] * 2, axis=0)
                values_ref[at] = values
    for at in range(16):
        values = values_ref[at]
        moves = moves_ref[at * 16 : (at + 1) * 16]
        near = moves & 127
        picked = [values[:, q : q + 128] for q in range(0, REACH, 128)]
        picked = [jnp.where(moves >= 128, b, a) for a, b in zip(picked[:-1], picked[1:])]
        picked = [jnp.where(lane < near, b, a) for a, b in zip(picked[:-1], picked[1:])]
        index = (lane + near) & 127
        result += jnp.concatenate([take(value, index) for value in picked], axis=1)
    out_ref[...] = result


def bring(*refs):
    half = len(refs) // 2
    for source, target in zip(refs[:half], refs[half:]):
        target[...] = source[...]


def brought(*values):
    return pl.pallas_call(
        bring,
        out_shape=[pltpu.VMEM(value.shape, value.dtype) for value in values],
        in_specs=[pl.BlockSpec(memory_space=pltpu.VMEM)] * len(values),
        out_specs=[pl.BlockSpec(memory_space=pltpu.VMEM)] * len(values),
    )(*values)


def local(records, templates, moveouts):
    i = lax.axis_index("tm")
    first = i % 2 == SENDER
    records, templates, moveouts = brought(
        jnp.transpose(records, (1, 0, 2)), jnp.transpose(templates, (0, 2, 1, 3)), jnp.transpose(moveouts)
    )
    packet = jnp.pad(jnp.transpose(templates, (2, 0, 1, 3)).reshape(16, 3 * LENGTH), ((0, 0), (0, TAPS - 3 * LENGTH)))
    series = jnp.pad(records.reshape(6, 512), ((0, 2), (0, TAPS - 512)))
    shifts = jnp.pad(moveouts.astype(jnp.bfloat16), ((0, 6), (0, TAPS - 128)))
    series = jnp.concatenate([series, shifts], axis=0)
    mine = jnp.where(first, packet, series)
    came = exchange(jnp.where(first, series, packet), other_core, other_core)
    three = exchange(mine, across_y, to_previous_across)
    held = jnp.concatenate([came[:8], mine[:8], came[8:], mine[8:]], axis=0)
    one = exchange(held, to_owner, to_previous)
    two = exchange(held, to_owner_across, across_high)
    order = arrangement()
    ends = i // 2 == 7
    near_after = jnp.where(ends, jnp.zeros_like(one[8:16]), one[8:16])
    far_after = jnp.where(ends, jnp.zeros_like(three[:8]), three[:8])
    near = jnp.where(first, one, jnp.concatenate([mine[:8], came[:8], near_after, mine[8:]], axis=0))
    far = jnp.where(first, two, jnp.concatenate([two[8:16], two[:8], far_after, two[24:]], axis=0))
    held = jnp.stack([near, far])
    held = jnp.stack([held] + [exchange(held, back_x(steps), back_z(steps)) for steps in (1, 2, 3)])
    held = jnp.stack([held, exchange(held, other_core, other_core)])

    return pl.pallas_call(
        kernel,
        out_shape=jax.ShapeDtypeStruct((16, 512), jnp.float32),
        in_specs=[pl.BlockSpec(memory_space=pltpu.VMEM)] * 2,
        out_specs=pl.BlockSpec(memory_space=pltpu.VMEM),
        scratch_shapes=[
            pltpu.VMEM((16, ROWS, REACH), jnp.float32),
            pltpu.VMEM((16, 3 * LAG, SPAN), jnp.bfloat16),
            pltpu.VMEM((256, PARTS * COLUMNS), jnp.bfloat16),
            pltpu.VMEM((256, 128), jnp.int32),
            pltpu.VMEM((256, 128), jnp.bfloat16),
            pltpu.VMEM((16, 16, REACH), jnp.float32),
        ],
        compiler_params=pltpu.CompilerParams(vmem_limit_bytes=40 * 1024 * 1024),
        cost_estimate=pl.CostEstimate(flops=2 * 128 * 2 * 600 * 696, bytes_accessed=600_000, transcendentals=0),
    )(held, order)


def solution(mesh):
    return jax.shard_map(
        local,
        mesh=mesh,
        in_specs=(P("sta", None, "tm"), P("tm", "sta", None, None), P(None, "sta")),
        out_specs=P("sta", "tm"),
        check_vma=False,
    )
```

```python
import jax
import jax.numpy as jnp
from jax import lax
from jax.experimental import pallas as pl
from jax.experimental.pallas import tpu as pltpu
from jax.sharding import PartitionSpec as P

EPS = 1e-06
LENGTH = 200
LAG = 64
REACH = 768
SPAN = 896
TAPS = 640
WIDE = 1024
ROWS = 8
SENDER = 1
PARTS = LENGTH // LAG + 1
GROUP = 128 // LAG
COLUMNS = 128 if 3 * LAG <= 128 else 256


def coordinates(time_index, station_index):
    return time_index // 4, (time_index // 2) % 2, time_index % 2, station_index // 4, station_index % 4


def exchange(value, templates_to, records_to):
    pairs = []
    for i in range(16):
        for j in range(8):
            target = (templates_to if i % 2 == SENDER else records_to)(*coordinates(i, j))
            x, y, core, high, z = target
            pairs.append((i * 8 + j, ((x * 2 + y) * 2 + core) * 8 + high * 4 + z))
    return lax.ppermute(value, ("tm", "sta"), pairs)


def other_core(x, y, core, high, z):
    return x, y, 1 - core, high, z


def to_owner(x, y, core, high, z):
    near, level = x // 2, x % 2 * 2 + y
    return (x + 2 + z - level) % 4, y ^ high ^ near, core, near, level


def to_previous(x, y, core, high, z):
    return (x - 1 + y) % 4, 1 - y, core, high, z


def to_owner_across(x, y, core, high, z):
    x, y, core, high, z = to_owner(x, y, core, high, z)
    return x, 1 - y, core, high, z


def to_previous_across(x, y, core, high, z):
    if x + y == 0:
        return x, y, 1 - core, high, z
    return x - 1 + y, 1 - y, core, 1 - high, z


def to_next(x, y, core, high, z):
    if x * 2 + y == 7:
        return x, y, 1 - core, high, z
    return x + y, 1 - y, core, high, z


def across_y(x, y, core, high, z):
    return x, 1 - y, core, high, z


def across_high(x, y, core, high, z):
    return x, y, core, 1 - high, z


def back_x(steps):
    return lambda x, y, core, high, z: ((x - steps) % 4, y, core, high, z)


def back_z(steps):
    return lambda x, y, core, high, z: (x, y, core, high, (z - steps) % 4)


def take(value, index):
    return jnp.take_along_axis(value, index, axis=1)


def windows(series):
    return pltpu.roll(series, WIDE - LAG + 1, 1, stride=1, stride_axis=0)[:, :SPAN].astype(jnp.bfloat16)


def ahead(value, steps):
    return pltpu.roll(value, value.shape[1] - steps, 1)


def arrangement():
    source = lax.broadcasted_iota(jnp.int32, (TAPS, PARTS * COLUMNS), 0)
    column = lax.broadcasted_iota(jnp.int32, (TAPS, PARTS * COLUMNS), 1)
    place = column % COLUMNS
    lag = column // COLUMNS * LAG + LAG - 1 - place % LAG
    wanted = place // LAG * LENGTH + lag
    return jnp.where((source == wanted) & (lag < LENGTH) & (place < 3 * LAG), 1.0, 0.0).astype(jnp.bfloat16)


def kernel(gathered_ref, arrangement_ref, out_ref, scale_ref, lagged_ref, left_ref, moves_ref, chosen_ref, values_ref):
    i, j = lax.axis_index("tm"), lax.axis_index("sta")
    x, y, core, _, z = coordinates(i, j)
    sender = jnp.where(core == SENDER, 0, 1)
    template = lax.broadcasted_iota(jnp.int32, (16, 128), 0)
    lane = lax.broadcasted_iota(jnp.int32, (16, 128), 1)
    own = lane == template + 16 * j
    energies = []
    for slot in range(8):
        level = lax.rem(x + slot // 2 - j // 2 + 6, 4)
        half = lax.rem(y + slot % 2 + j, 2)
        held = gathered_ref[1 - sender, level, half].astype(jnp.float32)
        pieces = [held[at : at + ROWS, :512] for at in (0, 8, 16)]
        wide = jnp.concatenate([jnp.where(core == 0, a, b) for a, b in zip(pieces[:-1], pieces[1:])], axis=1)
        squares = wide * wide
        energies.append(squares[0:2] + squares[2:4] + squares[4:6])
        for station in range(2):
            at = slot * 2 + station
            shifts = jnp.broadcast_to(held[24 + station : 25 + station, :128], (16, 128))
            chosen_ref[at * 16 : (at + 1) * 16] = jnp.where(own, shifts, 0.0).astype(jnp.bfloat16)
            for c in range(3):
                row = jnp.broadcast_to(wide[c * 2 + station : c * 2 + station + 1], (LAG, WIDE))
                lagged_ref[at, c * LAG : (c + 1) * LAG] = windows(row)
    energy = jnp.concatenate(energies, axis=0)
    four = energy + ahead(energy, 1) + (ahead(energy, 2) + ahead(energy, 3))
    eight = four + ahead(four, 4)
    sixteen = eight + (ahead(four, 8) + ahead(four, 12))
    sixty = sixteen + ahead(sixteen, 16) + (ahead(sixteen, 32) + ahead(sixteen, 48))
    total = sixty + ahead(sixty, 64) + (ahead(sixty, 128) + ahead(eight, 192))
    scale = lax.rsqrt(total[:, :REACH] + EPS)
    for row in range(16):
        scale_ref[row] = jnp.broadcast_to(scale[row : row + 1], (ROWS, REACH))

    moves_ref[...] = jnp.dot(
        chosen_ref[...], jnp.ones((128, 128), jnp.bfloat16), preferred_element_type=jnp.float32
    ).astype(jnp.int32)
    blocks = gathered_ref[sender].reshape(256, TAPS)
    left_ref[...] = jnp.dot(blocks, arrangement_ref[...], preferred_element_type=jnp.float32).astype(jnp.bfloat16)

    result = jnp.zeros((16, 512), jnp.float32)
    for dx in range(4):
        for dy in range(2):
            for station in range(2):
                at = (dx * 2 + dy) * 2 + station
                top = at * 16
                left = jnp.concatenate(
                    [left_ref[top : top + 16, a * COLUMNS : a * COLUMNS + 3 * LAG] for a in range(PARTS)], axis=0
                )
                sums = jnp.dot(left, lagged_ref[at], preferred_element_type=jnp.float32)
                parts = [sums[a * 16 : (a + 1) * 16] for a in range(PARTS)]
                values = None
                for group in range(GROUP - 1, -1, -1):
                    term = parts[group]
                    if group + GROUP < PARTS:
                        term = term[:, :REACH] + parts[group + GROUP][:, 128:]
                    values = term if values is None else term + ahead(values, LAG)[:, :REACH]
                values = values * jnp.concatenate([scale_ref[at]] * 2, axis=0)
                values_ref[at] = values
    for at in range(16):
        values = values_ref[at]
        moves = moves_ref[at * 16 : (at + 1) * 16]
        near = moves & 127
        picked = [values[:, q : q + 128] for q in range(0, REACH, 128)]
        picked = [jnp.where(moves >= 128, b, a) for a, b in zip(picked[:-1], picked[1:])]
        picked = [jnp.where(lane < near, b, a) for a, b in zip(picked[:-1], picked[1:])]
        index = (lane + near) & 127
        result += jnp.concatenate([take(value, index) for value in picked], axis=1)
    out_ref[...] = result


def bring(*refs):
    half = len(refs) // 2
    for source, target in zip(refs[:half], refs[half:]):
        target[...] = source[...]


def brought(*values):
    return pl.pallas_call(
        bring,
        out_shape=[pltpu.VMEM(value.shape, value.dtype) for value in values],
        in_specs=[pl.BlockSpec(memory_space=pltpu.VMEM)] * len(values),
        out_specs=[pl.BlockSpec(memory_space=pltpu.VMEM)] * len(values),
    )(*values)


def local(records, templates, moveouts):
    i = lax.axis_index("tm")
    first = i % 2 == SENDER
    records, templates, moveouts = brought(
        jnp.transpose(records, (1, 0, 2)), jnp.transpose(templates, (0, 2, 1, 3)), jnp.transpose(moveouts)
    )
    packet = jnp.pad(jnp.transpose(templates, (2, 0, 1, 3)).reshape(16, 3 * LENGTH), ((0, 0), (0, TAPS - 3 * LENGTH)))
    series = jnp.pad(records.reshape(6, 512), ((0, 2), (0, TAPS - 512)))
    shifts = jnp.pad(moveouts.astype(jnp.bfloat16), ((0, 6), (0, TAPS - 128)))
    series = jnp.concatenate([series, shifts], axis=0)
    mine = jnp.where(first, packet, series)
    came = exchange(jnp.where(first, series, packet), other_core, other_core)
    three = exchange(mine, to_next, to_previous_across)
    held = jnp.concatenate([came[:8], mine[:8], came[8:], mine[8:]], axis=0)
    one = exchange(held, to_owner, to_previous)
    two = exchange(held, to_owner_across, across_high)
    order = arrangement()
    ends = i // 2 == 7
    near_after = jnp.where(ends, jnp.zeros_like(one[8:16]), one[8:16])
    far_after = jnp.where(ends, jnp.zeros_like(three[:8]), three[:8])
    near = jnp.where(first, one, jnp.concatenate([mine[:8], came[:8], near_after, mine[8:]], axis=0))
    far = jnp.where(first, two, jnp.concatenate([two[8:16], two[:8], far_after, two[24:]], axis=0))
    held = jnp.stack([near, far])
    held = jnp.stack([held] + [exchange(held, back_x(steps), back_z(steps)) for steps in (1, 2, 3)])
    held = jnp.stack([held, exchange(held, other_core, other_core)])

    return pl.pallas_call(
        kernel,
        out_shape=jax.ShapeDtypeStruct((16, 512), jnp.float32),
        in_specs=[pl.BlockSpec(memory_space=pltpu.VMEM)] * 2,
        out_specs=pl.BlockSpec(memory_space=pltpu.VMEM),
        scratch_shapes=[
            pltpu.VMEM((16, ROWS, REACH), jnp.float32),
            pltpu.VMEM((16, 3 * LAG, SPAN), jnp.bfloat16),
            pltpu.VMEM((256, PARTS * COLUMNS), jnp.bfloat16),
            pltpu.VMEM((256, 128), jnp.int32),
            pltpu.VMEM((256, 128), jnp.bfloat16),
            pltpu.VMEM((16, 16, REACH), jnp.float32),
        ],
        compiler_params=pltpu.CompilerParams(vmem_limit_bytes=40 * 1024 * 1024),
        cost_estimate=pl.CostEstimate(flops=2 * 128 * 2 * 600 * 696, bytes_accessed=600_000, transcendentals=0),
    )(held, order)


def solution(mesh):
    return jax.shard_map(
        local,
        mesh=mesh,
        in_specs=(P("sta", None, "tm"), P("tm", "sta", None, None), P(None, "sta")),
        out_specs=P("sta", "tm"),
        check_vma=False,
    )
```

```python
import jax
import jax.numpy as jnp
from jax import lax
from jax.experimental import pallas as pl
from jax.experimental.pallas import tpu as pltpu
from jax.sharding import PartitionSpec as P

EPS = 1e-06
LENGTH = 200
LAG = 64
REACH = 768
SPAN = 896
TAPS = 640
WIDE = 1024
ROWS = 8
SENDER = 1
PARTS = LENGTH // LAG + 1
GROUP = 128 // LAG
COLUMNS = 128 if 3 * LAG <= 128 else 256


def coordinates(time_index, station_index):
    return time_index // 4, (time_index // 2) % 2, time_index % 2, station_index // 4, station_index % 4


def exchange(value, templates_to, records_to):
    pairs = []
    for i in range(16):
        for j in range(8):
            target = (templates_to if i % 2 == SENDER else records_to)(*coordinates(i, j))
            x, y, core, high, z = target
            pairs.append((i * 8 + j, ((x * 2 + y) * 2 + core) * 8 + high * 4 + z))
    return lax.ppermute(value, ("tm", "sta"), pairs)


def other_core(x, y, core, high, z):
    return x, y, 1 - core, high, z


def to_owner(x, y, core, high, z):
    near, level = x // 2, x % 2 * 2 + y
    return (x + 2 + z - level) % 4, y ^ high ^ near, core, near, level


def to_previous(x, y, core, high, z):
    return (x - 1 + y) % 4, 1 - y, core, high, z


def to_owner_across(x, y, core, high, z):
    x, y, core, high, z = to_owner(x, y, core, high, z)
    return x, 1 - y, core, high, z


def to_previous_across(x, y, core, high, z):
    if x + y == 0:
        return x, y, 1 - core, high, z
    return x - 1 + y, 1 - y, core, 1 - high, z


def to_next(x, y, core, high, z):
    if x * 2 + y == 7:
        return x, y, 1 - core, high, z
    return x + y, 1 - y, core, high, z


def across_y(x, y, core, high, z):
    return x, 1 - y, core, high, z


def across_high(x, y, core, high, z):
    return x, y, core, 1 - high, z


def back_x(steps):
    return lambda x, y, core, high, z: ((x - steps) % 4, y, core, high, z)


def back_z(steps):
    return lambda x, y, core, high, z: (x, y, core, high, (z - steps) % 4)


def take(value, index):
    return jnp.take_along_axis(value, index, axis=1)


def windows(series):
    return pltpu.roll(series, WIDE - LAG + 1, 1, stride=1, stride_axis=0)[:, :SPAN].astype(jnp.bfloat16)


def ahead(value, steps):
    return pltpu.roll(value, value.shape[1] - steps, 1)


def arrangement():
    source = lax.broadcasted_iota(jnp.int32, (TAPS, PARTS * COLUMNS), 0)
    column = lax.broadcasted_iota(jnp.int32, (TAPS, PARTS * COLUMNS), 1)
    place = column % COLUMNS
    lag = column // COLUMNS * LAG + LAG - 1 - place % LAG
    wanted = place // LAG * LENGTH + lag
    return jnp.where((source == wanted) & (lag < LENGTH) & (place < 3 * LAG), 1.0, 0.0).astype(jnp.bfloat16)


def kernel(gathered_ref, arrangement_ref, out_ref, scale_ref, lagged_ref, left_ref, moves_ref, chosen_ref, values_ref):
    i, j = lax.axis_index("tm"), lax.axis_index("sta")
    x, y, core, _, z = coordinates(i, j)
    sender = jnp.where(core == SENDER, 0, 1)
    template = lax.broadcasted_iota(jnp.int32, (16, 128), 0)
    lane = lax.broadcasted_iota(jnp.int32, (16, 128), 1)
    own = lane == template + 16 * j
    energies = []
    for slot in range(8):
        level = lax.rem(x - slot // 2 - j // 2 + 10, 4)
        half = lax.rem(y + slot % 2 + j, 2)
        held = gathered_ref[1 - sender, level, half].astype(jnp.float32)
        pieces = [held[at : at + ROWS, :512] for at in (0, 8, 16)]
        wide = jnp.concatenate([jnp.where(core == 0, a, b) for a, b in zip(pieces[:-1], pieces[1:])], axis=1)
        squares = wide * wide
        energies.append(squares[0:2] + squares[2:4] + squares[4:6])
        for station in range(2):
            at = slot * 2 + station
            shifts = jnp.broadcast_to(held[24 + station : 25 + station, :128], (16, 128))
            chosen_ref[at * 16 : (at + 1) * 16] = jnp.where(own, shifts, 0.0).astype(jnp.bfloat16)
            for c in range(3):
                row = jnp.broadcast_to(wide[c * 2 + station : c * 2 + station + 1], (LAG, WIDE))
                lagged_ref[at, c * LAG : (c + 1) * LAG] = windows(row)
    energy = jnp.concatenate(energies, axis=0)
    four = energy + ahead(energy, 1) + (ahead(energy, 2) + ahead(energy, 3))
    eight = four + ahead(four, 4)
    sixteen = eight + (ahead(four, 8) + ahead(four, 12))
    sixty = sixteen + ahead(sixteen, 16) + (ahead(sixteen, 32) + ahead(sixteen, 48))
    total = sixty + ahead(sixty, 64) + (ahead(sixty, 128) + ahead(eight, 192))
    scale = lax.rsqrt(total[:, :REACH] + EPS)
    for row in range(16):
        scale_ref[row] = jnp.broadcast_to(scale[row : row + 1], (ROWS, REACH))

    moves_ref[...] = jnp.dot(
        chosen_ref[...], jnp.ones((128, 128), jnp.bfloat16), preferred_element_type=jnp.float32
    ).astype(jnp.int32)
    blocks = gathered_ref[sender].reshape(256, TAPS)
    left_ref[...] = jnp.dot(blocks, arrangement_ref[...], preferred_element_type=jnp.float32).astype(jnp.bfloat16)

    result = jnp.zeros((16, 512), jnp.float32)
    for dx in range(4):
        for dy in range(2):
            for station in range(2):
                at = (dx * 2 + dy) * 2 + station
                top = at * 16
                left = jnp.concatenate(
                    [left_ref[top : top + 16, a * COLUMNS : a * COLUMNS + 3 * LAG] for a in range(PARTS)], axis=0
                )
                sums = jnp.dot(left, lagged_ref[at], preferred_element_type=jnp.float32)
                parts = [sums[a * 16 : (a + 1) * 16] for a in range(PARTS)]
                values = None
                for group in range(GROUP - 1, -1, -1):
                    term = parts[group]
                    if group + GROUP < PARTS:
                        term = term[:, :REACH] + parts[group + GROUP][:, 128:]
                    values = term if values is None else term + ahead(values, LAG)[:, :REACH]
                values = values * jnp.concatenate([scale_ref[at]] * 2, axis=0)
                values_ref[at] = values
    for at in range(16):
        values = values_ref[at]
        moves = moves_ref[at * 16 : (at + 1) * 16]
        near = moves & 127
        picked = [values[:, q : q + 128] for q in range(0, REACH, 128)]
        picked = [jnp.where(moves >= 128, b, a) for a, b in zip(picked[:-1], picked[1:])]
        picked = [jnp.where(lane < near, b, a) for a, b in zip(picked[:-1], picked[1:])]
        index = (lane + near) & 127
        result += jnp.concatenate([take(value, index) for value in picked], axis=1)
    out_ref[...] = result


def bring(*refs):
    half = len(refs) // 2
    for source, target in zip(refs[:half], refs[half:]):
        target[...] = source[...]


def brought(*values):
    return pl.pallas_call(
        bring,
        out_shape=[pltpu.VMEM(value.shape, value.dtype) for value in values],
        in_specs=[pl.BlockSpec(memory_space=pltpu.VMEM)] * len(values),
        out_specs=[pl.BlockSpec(memory_space=pltpu.VMEM)] * len(values),
    )(*values)


def local(records, templates, moveouts):
    i = lax.axis_index("tm")
    first = i % 2 == SENDER
    records, templates, moveouts = brought(
        jnp.transpose(records, (1, 0, 2)), jnp.transpose(templates, (0, 2, 1, 3)), jnp.transpose(moveouts)
    )
    packet = jnp.pad(jnp.transpose(templates, (2, 0, 1, 3)).reshape(16, 3 * LENGTH), ((0, 0), (0, TAPS - 3 * LENGTH)))
    series = jnp.pad(records.reshape(6, 512), ((0, 2), (0, TAPS - 512)))
    shifts = jnp.pad(moveouts.astype(jnp.bfloat16), ((0, 6), (0, TAPS - 128)))
    series = jnp.concatenate([series, shifts], axis=0)
    mine = jnp.where(first, packet, series)
    came = exchange(jnp.where(first, series, packet), other_core, other_core)
    three = exchange(mine, to_next, to_previous_across)
    held = jnp.concatenate([came[:8], mine[:8], came[8:], mine[8:]], axis=0)
    one = exchange(held, to_owner, to_previous)
    two = exchange(held, to_owner_across, across_high)
    order = arrangement()
    ends = i // 2 == 7
    near_after = jnp.where(ends, jnp.zeros_like(one[8:16]), one[8:16])
    far_after = jnp.where(ends, jnp.zeros_like(three[:8]), three[:8])
    near = jnp.where(first, one, jnp.concatenate([mine[:8], came[:8], near_after, mine[8:]], axis=0))
    far = jnp.where(first, two, jnp.concatenate([two[8:16], two[:8], far_after, two[24:]], axis=0))
    held = jnp.stack([near, far])
    held = jnp.stack([held] + [exchange(held, back_x(-steps), back_z(steps)) for steps in (1, 2, 3)])
    held = jnp.stack([held, exchange(held, other_core, other_core)])

    return pl.pallas_call(
        kernel,
        out_shape=jax.ShapeDtypeStruct((16, 512), jnp.float32),
        in_specs=[pl.BlockSpec(memory_space=pltpu.VMEM)] * 2,
        out_specs=pl.BlockSpec(memory_space=pltpu.VMEM),
        scratch_shapes=[
            pltpu.VMEM((16, ROWS, REACH), jnp.float32),
            pltpu.VMEM((16, 3 * LAG, SPAN), jnp.bfloat16),
            pltpu.VMEM((256, PARTS * COLUMNS), jnp.bfloat16),
            pltpu.VMEM((256, 128), jnp.int32),
            pltpu.VMEM((256, 128), jnp.bfloat16),
            pltpu.VMEM((16, 16, REACH), jnp.float32),
        ],
        compiler_params=pltpu.CompilerParams(vmem_limit_bytes=40 * 1024 * 1024),
        cost_estimate=pl.CostEstimate(flops=2 * 128 * 2 * 600 * 696, bytes_accessed=600_000, transcendentals=0),
    )(held, order)


def solution(mesh):
    return jax.shard_map(
        local,
        mesh=mesh,
        in_specs=(P("sta", None, "tm"), P("tm", "sta", None, None), P(None, "sta")),
        out_specs=P("sta", "tm"),
        check_vma=False,
    )
```

```python
import jax
import jax.numpy as jnp
from jax import lax
from jax.experimental import pallas as pl
from jax.experimental.pallas import tpu as pltpu
from jax.sharding import PartitionSpec as P

EPS = 1e-06
LENGTH = 200
LAG = 64
REACH = 768
SPAN = 896
TAPS = 640
WIDE = 1024
ROWS = 8
SENDER = 1
PARTS = LENGTH // LAG + 1
GROUP = 128 // LAG
COLUMNS = 128 if 3 * LAG <= 128 else 256


def coordinates(time_index, station_index):
    return time_index // 4, (time_index // 2) % 2, time_index % 2, station_index // 4, station_index % 4


def exchange(value, templates_to, records_to):
    pairs = []
    for i in range(16):
        for j in range(8):
            target = (templates_to if i % 2 == SENDER else records_to)(*coordinates(i, j))
            x, y, core, high, z = target
            pairs.append((i * 8 + j, ((x * 2 + y) * 2 + core) * 8 + high * 4 + z))
    return lax.ppermute(value, ("tm", "sta"), pairs)


def other_core(x, y, core, high, z):
    return x, y, 1 - core, high, z


def to_owner(x, y, core, high, z):
    near, level = x // 2, x % 2 * 2 + y
    return (x + 2 + z - level) % 4, y ^ high ^ near, core, near, level


def to_previous(x, y, core, high, z):
    return (x - 1 + y) % 4, 1 - y, core, high, z


def to_owner_across(x, y, core, high, z):
    x, y, core, high, z = to_owner(x, y, core, high, z)
    return x, 1 - y, core, high, z


def to_previous_across(x, y, core, high, z):
    if x + y == 0:
        return x, y, 1 - core, high, z
    return x - 1 + y, 1 - y, core, 1 - high, z


def to_next(x, y, core, high, z):
    if x * 2 + y == 7:
        return x, y, 1 - core, high, z
    return x + y, 1 - y, core, high, z


def across_y(x, y, core, high, z):
    return x, 1 - y, core, high, z


def across_high(x, y, core, high, z):
    return x, y, core, 1 - high, z


def back_x(steps):
    return lambda x, y, core, high, z: ((x - steps) % 4, y, core, high, z)


def back_z(steps):
    return lambda x, y, core, high, z: (x, y, core, high, (z - steps) % 4)


def take(value, index):
    return jnp.take_along_axis(value, index, axis=1)


def windows(series):
    return pltpu.roll(series, WIDE - LAG + 1, 1, stride=1, stride_axis=0)[:, :SPAN].astype(jnp.bfloat16)


def ahead(value, steps):
    return pltpu.roll(value, value.shape[1] - steps, 1)


def arrangement():
    source = lax.broadcasted_iota(jnp.int32, (TAPS, PARTS * COLUMNS), 0)
    column = lax.broadcasted_iota(jnp.int32, (TAPS, PARTS * COLUMNS), 1)
    place = column % COLUMNS
    lag = column // COLUMNS * LAG + LAG - 1 - place % LAG
    wanted = place // LAG * LENGTH + lag
    return jnp.where((source == wanted) & (lag < LENGTH) & (place < 3 * LAG), 1.0, 0.0).astype(jnp.bfloat16)


def kernel(gathered_ref, arrangement_ref, out_ref, scale_ref, lagged_ref, left_ref, moves_ref, chosen_ref, values_ref):
    i, j = lax.axis_index("tm"), lax.axis_index("sta")
    x, y, core, _, z = coordinates(i, j)
    sender = jnp.where(core == SENDER, 0, 1)
    template = lax.broadcasted_iota(jnp.int32, (16, 128), 0)
    lane = lax.broadcasted_iota(jnp.int32, (16, 128), 1)
    own = lane == template + 16 * j
    energies = []
    for slot in range(8):
        level = lax.rem(j // 2 - x + slot // 2 + 6, 4)
        half = lax.rem(y + slot % 2 + j, 2)
        held = gathered_ref[1 - sender, level, half].astype(jnp.float32)
        pieces = [held[at : at + ROWS, :512] for at in (0, 8, 16)]
        wide = jnp.concatenate([jnp.where(core == 0, a, b) for a, b in zip(pieces[:-1], pieces[1:])], axis=1)
        squares = wide * wide
        energies.append(squares[0:2] + squares[2:4] + squares[4:6])
        for station in range(2):
            at = slot * 2 + station
            shifts = jnp.broadcast_to(held[24 + station : 25 + station, :128], (16, 128))
            chosen_ref[at * 16 : (at + 1) * 16] = jnp.where(own, shifts, 0.0).astype(jnp.bfloat16)
            for c in range(3):
                row = jnp.broadcast_to(wide[c * 2 + station : c * 2 + station + 1], (LAG, WIDE))
                lagged_ref[at, c * LAG : (c + 1) * LAG] = windows(row)
    energy = jnp.concatenate(energies, axis=0)
    four = energy + ahead(energy, 1) + (ahead(energy, 2) + ahead(energy, 3))
    eight = four + ahead(four, 4)
    sixteen = eight + (ahead(four, 8) + ahead(four, 12))
    sixty = sixteen + ahead(sixteen, 16) + (ahead(sixteen, 32) + ahead(sixteen, 48))
    total = sixty + ahead(sixty, 64) + (ahead(sixty, 128) + ahead(eight, 192))
    scale = lax.rsqrt(total[:, :REACH] + EPS)
    for row in range(16):
        scale_ref[row] = jnp.broadcast_to(scale[row : row + 1], (ROWS, REACH))

    moves_ref[...] = jnp.dot(
        chosen_ref[...], jnp.ones((128, 128), jnp.bfloat16), preferred_element_type=jnp.float32
    ).astype(jnp.int32)
    blocks = gathered_ref[sender].reshape(256, TAPS)
    left_ref[...] = jnp.dot(blocks, arrangement_ref[...], preferred_element_type=jnp.float32).astype(jnp.bfloat16)

    result = jnp.zeros((16, 512), jnp.float32)
    for dx in range(4):
        for dy in range(2):
            for station in range(2):
                at = (dx * 2 + dy) * 2 + station
                top = at * 16
                left = jnp.concatenate(
                    [left_ref[top : top + 16, a * COLUMNS : a * COLUMNS + 3 * LAG] for a in range(PARTS)], axis=0
                )
                sums = jnp.dot(left, lagged_ref[at], preferred_element_type=jnp.float32)
                parts = [sums[a * 16 : (a + 1) * 16] for a in range(PARTS)]
                values = None
                for group in range(GROUP - 1, -1, -1):
                    term = parts[group]
                    if group + GROUP < PARTS:
                        term = term[:, :REACH] + parts[group + GROUP][:, 128:]
                    values = term if values is None else term + ahead(values, LAG)[:, :REACH]
                values = values * jnp.concatenate([scale_ref[at]] * 2, axis=0)
                values_ref[at] = values
    for at in range(16):
        values = values_ref[at]
        moves = moves_ref[at * 16 : (at + 1) * 16]
        near = moves & 127
        picked = [values[:, q : q + 128] for q in range(0, REACH, 128)]
        picked = [jnp.where(moves >= 128, b, a) for a, b in zip(picked[:-1], picked[1:])]
        picked = [jnp.where(lane < near, b, a) for a, b in zip(picked[:-1], picked[1:])]
        index = (lane + near) & 127
        result += jnp.concatenate([take(value, index) for value in picked], axis=1)
    out_ref[...] = result


def bring(*refs):
    half = len(refs) // 2
    for source, target in zip(refs[:half], refs[half:]):
        target[...] = source[...]


def brought(*values):
    return pl.pallas_call(
        bring,
        out_shape=[pltpu.VMEM(value.shape, value.dtype) for value in values],
        in_specs=[pl.BlockSpec(memory_space=pltpu.VMEM)] * len(values),
        out_specs=[pl.BlockSpec(memory_space=pltpu.VMEM)] * len(values),
    )(*values)


def local(records, templates, moveouts):
    i = lax.axis_index("tm")
    first = i % 2 == SENDER
    records, templates, moveouts = brought(
        jnp.transpose(records, (1, 0, 2)), jnp.transpose(templates, (0, 2, 1, 3)), jnp.transpose(moveouts)
    )
    packet = jnp.pad(jnp.transpose(templates, (2, 0, 1, 3)).reshape(16, 3 * LENGTH), ((0, 0), (0, TAPS - 3 * LENGTH)))
    series = jnp.pad(records.reshape(6, 512), ((0, 2), (0, TAPS - 512)))
    shifts = jnp.pad(moveouts.astype(jnp.bfloat16), ((0, 6), (0, TAPS - 128)))
    series = jnp.concatenate([series, shifts], axis=0)
    mine = jnp.where(first, packet, series)
    came = exchange(jnp.where(first, series, packet), other_core, other_core)
    three = exchange(mine, to_next, to_previous_across)
    held = jnp.concatenate([came[:8], mine[:8], came[8:], mine[8:]], axis=0)
    one = exchange(held, to_owner, to_previous)
    two = exchange(held, to_owner_across, across_high)
    order = arrangement()
    ends = i // 2 == 7
    near_after = jnp.where(ends, jnp.zeros_like(one[8:16]), one[8:16])
    far_after = jnp.where(ends, jnp.zeros_like(three[:8]), three[:8])
    near = jnp.where(first, one, jnp.concatenate([mine[:8], came[:8], near_after, mine[8:]], axis=0))
    far = jnp.where(first, two, jnp.concatenate([two[8:16], two[:8], far_after, two[24:]], axis=0))
    held = jnp.stack([near, far])
    held = jnp.stack([held] + [exchange(held, back_x(-steps), back_z(-steps)) for steps in (1, 2, 3)])
    held = jnp.stack([held, exchange(held, other_core, other_core)])

    return pl.pallas_call(
        kernel,
        out_shape=jax.ShapeDtypeStruct((16, 512), jnp.float32),
        in_specs=[pl.BlockSpec(memory_space=pltpu.VMEM)] * 2,
        out_specs=pl.BlockSpec(memory_space=pltpu.VMEM),
        scratch_shapes=[
            pltpu.VMEM((16, ROWS, REACH), jnp.float32),
            pltpu.VMEM((16, 3 * LAG, SPAN), jnp.bfloat16),
            pltpu.VMEM((256, PARTS * COLUMNS), jnp.bfloat16),
            pltpu.VMEM((256, 128), jnp.int32),
            pltpu.VMEM((256, 128), jnp.bfloat16),
            pltpu.VMEM((16, 16, REACH), jnp.float32),
        ],
        compiler_params=pltpu.CompilerParams(vmem_limit_bytes=40 * 1024 * 1024),
        cost_estimate=pl.CostEstimate(flops=2 * 128 * 2 * 600 * 696, bytes_accessed=600_000, transcendentals=0),
    )(held, order)


def solution(mesh):
    return jax.shard_map(
        local,
        mesh=mesh,
        in_specs=(P("sta", None, "tm"), P("tm", "sta", None, None), P(None, "sta")),
        out_specs=P("sta", "tm"),
        check_vma=False,
    )
```
